128 devices in a mesh: tm: 4 (over z), det: 32 (over y, x, core).
Axes of the slice: x: 4, y: 4, z: 4, core: 2. Of those that a mesh axis runs over, the one named last changes fastest.
Arguments:
- time_stream: bfloat16 [1024, 131072], P('det', 'tm'), may hold values from -6 to 6
- filter_taps: bfloat16 [1024, 129], P('det'), may hold values from -0.5 to 0.5
- det_precision: bfloat16 [1024, 1024], replicated
- left_weight: float32 [128, 32], replicated, may hold values from -0.046875 to 0.046875
- right_weight: float32 [128, 32], replicated, may hold values from -1 to 1
- frame_tile: int32 [131072, 1], P(('tm', 'det')), may hold values from 0 to 255; in each aligned block of 1024 rows (0 to 1023, 1024 to 2047, ...) at most 6 rows name the same one
- tile_owner: int32 [256], replicated, may hold values from 0 to 127, as said below
- frame_count: int32 [128], P(('tm', 'det')), may hold values from 512 to 1024, as said below
Outputs:
- sky_map: float32 [256, 16384], P(('tm', 'det'))
The draws below stay inside these ranges and needn't reach their ends.
Inputs may be any that keep to these rules, and one draw needn't show every extreme that they name: `frame_tile`: within the frames of one segment (aligned blocks of 1024 rows) no tile is named more than 6 times, a bound that some block reaches. `tile_owner`: every device number is the owner of exactly 2 tiles. `frame_count`: some segment has all 1024 frames live.
All inputs are finite; a program needn't handle non-finite values.
Results may differ from the reference program's by a relative error of at most 0.0041.
Values may be sent and summed in bfloat16 or wider, within the bound.
No kernel may reach another device: no remote copies, remote signals or barrier semaphores. Data moves between devices by JAX's collectives and lax.ppermute only.
A program may use at most 64 MiB of HBM per device.

```python
import math
import jax
import jax.numpy as jnp
import numpy as np
from jax import lax

NDET = 1024
HW = 64
FD = 32
FT = 32
TL = 128
SPAN = 1024
TILE_DEV = 2
TAPS = 129
NSAMP = 131072
F_DEV = 1024
NFRAMES = 131072
NTILES = 256
CAP = 6
N_TM = 4
N_DET = 32


def draw_det_precision(key, part):
    first_key, second_key = jax.random.split(jax.random.fold_in(key, 11))
    noise = jax.random.normal(first_key, (NDET, NDET), jnp.float32) * 0.02
    noise = (noise + noise.T) * 0.7071
    diagonal = jax.random.uniform(second_key, (NDET,), jnp.float32, 0.5, 1.5)
    matrix = noise + jnp.diag(diagonal)
    return matrix.astype(jnp.bfloat16)


def draw_tile_owner(key, part):
    order = jax.random.permutation(jax.random.fold_in(key, 23), NTILES)
    return (order // TILE_DEV).astype(jnp.int32)


def draw_frame_count(key, part):
    first_key, second_key = jax.random.split(jax.random.fold_in(key, 37))
    counts = jax.random.randint(first_key, (N_TM * N_DET,), F_DEV // 2, F_DEV + 1, dtype=jnp.int32)
    chosen = jax.random.randint(second_key, (), 0, N_TM * N_DET, dtype=jnp.int32)
    return counts.at[chosen].set(F_DEV).astype(jnp.int32)


def shard_levels(key, dims, cuts, smallest, top_value):
    level = 1.0
    for axis_at, parts in cuts:
        heights = jax.random.uniform(jax.random.fold_in(jax.random.fold_in(key, 6), axis_at), (parts,), jnp.float32, smallest / len(cuts), top_value / len(cuts))
        level = level * jnp.repeat(jnp.exp(heights), dims[axis_at] // parts).reshape((-1,) + (1,) * (len(dims) - 1 - axis_at))
    return level


def routed_block(key, own, number, rows, amount, top, limit, lean):
    ranking = jax.random.permutation(key, amount)
    crowded, usual = load_shares(amount, rows * top, limit, lean, True), load_shares(amount, rows * top, limit, lean, False)
    places = jnp.arange(amount)

    def named(tallies, offset_by):
        used = int((tallies > 0).sum())
        fixed = max(1, used // 4)
        passed = fixed + (places - fixed + offset_by * (used - fixed)) % max(1, amount - fixed)
        return jnp.zeros((amount,), jnp.int32).at[ranking[jnp.where(places < fixed, places, passed)]].set(jnp.asarray(tallies, jnp.int32))

    tallies = jnp.where(number % 4 == 0, named(crowded, number // 4), named(usual, number - number // 4 - 1))
    mixed = jax.random.permutation(jax.random.fold_in(own, 3), amount)
    giver, receiver = mixed[0:amount // 2 * 2:2], mixed[1:amount // 2 * 2:2]
    margin = jnp.minimum(tallies[giver] - 1, limit - tallies[receiver]) // 2
    margin = jnp.where((giver == ranking[0]) | (receiver == ranking[0]) | (tallies[receiver] == 0), 0, jnp.maximum(margin, 0))
    passed = jax.random.randint(jax.random.fold_in(own, 4), (amount // 2,), 0, 1 << 20) % (margin + 1)
    tallies = tallies.at[giver].add(-passed).at[receiver].add(passed)
    members = jnp.searchsorted(jnp.cumsum(tallies), jnp.arange(rows * top), side="right").astype(jnp.int32)
    table = members.reshape(top, rows).T
    table = table[jax.random.permutation(jax.random.fold_in(own, 1), rows)]
    offset_by = jax.random.randint(jax.random.fold_in(own, 2), (rows, 1), 0, top)
    return jnp.take_along_axis(table, (jnp.arange(top)[None, :] + offset_by) % top, axis=1)


def load_shares(number_of, total, limit, lean, full):
    portions = [(1 << 20) // math.isqrt(grade ** lean) + 1 for grade in range(1, number_of + 1)]
    largest = limit if full else min(limit, max(-(-total // number_of), total * portions[0] // sum(portions)))
    least = 1 if total - largest >= number_of - 1 else 0
    holding, rest = [largest] + [least] * (number_of - 1), total - largest - least * (number_of - 1)
    while rest > 0:
        candidates = [i for i in range(1, number_of) if holding[i] < largest] or [i for i in range(1, number_of) if holding[i] < limit]
        mass, remaining = sum([portions[i] for i in candidates]), rest
        for i in candidates:
            addition = min(limit - holding[i], max(1, remaining * portions[i] // mass), rest)
            holding[i] = holding[i] + addition
            rest = rest - addition
    return np.array(holding)


def centred(stream_key, dims, scale, limit, cuts=(), kind=jnp.bfloat16):
    gain = shard_levels(stream_key, dims, cuts, -0.22, 0.18) if cuts else 1.0
    values = jax.random.normal(stream_key, dims, jnp.float32) * scale * gain
    return jnp.minimum(jnp.maximum(values, -limit), limit).astype(kind)


def setup_inputs(seed: int = 0) -> dict:
    key_list = jax.random.split(jax.random.key(seed), 9)
    time_stream = centred(key_list[0], (NDET, NSAMP), 1.0, 6.0, ((0, 32), (1, 4)))
    filter_taps = centred(key_list[1], (NDET, TAPS), TAPS ** -0.5, 0.5, ((0, 32),))
    det_precision = draw_det_precision(jax.random.fold_in(key_list[8], 71), 0)
    left_weight = centred(key_list[3], (TL, FD), (FD * F_DEV // TILE_DEV) ** -0.5, 0.046875, (), jnp.float32)
    right_weight = centred(key_list[4], (TL, FT), FT ** -0.5, 1.0, (), jnp.float32)
    frame_tile_keys = jax.random.split(jax.random.fold_in(key_list[5], 1), NFRAMES // F_DEV)
    frame_tile_turns = jax.random.permutation(jax.random.fold_in(key_list[5], 3), NFRAMES // F_DEV)
    frame_tile = jax.vmap(lambda own, number: routed_block(jax.random.fold_in(key_list[5], 2), own, number, F_DEV, NTILES, 1, CAP, 2))(frame_tile_keys, frame_tile_turns).reshape((NFRAMES, 1))
    tile_owner = draw_tile_owner(jax.random.fold_in(key_list[8], 71), 0)
    frame_count = draw_frame_count(jax.random.fold_in(key_list[8], 71), 0)
    return {"time_stream": time_stream, "filter_taps": filter_taps, "det_precision": det_precision, "left_weight": left_weight, "right_weight": right_weight, "frame_tile": frame_tile, "tile_owner": tile_owner, "frame_count": frame_count}


def toeplitz_block(filter_taps, half_width):
    row_index = jnp.arange(4 * half_width, dtype=jnp.int32)[:, None]
    col_index = jnp.arange(2 * half_width, dtype=jnp.int32)[None, :]
    offset = row_index - col_index
    inside = (offset >= 0) & (offset <= 2 * half_width)
    picked = jnp.take(filter_taps, jnp.clip(offset, 0, 2 * half_width), axis=1)
    return jnp.where(inside[None, :, :], picked, jnp.zeros((), filter_taps.dtype))


def apply_filter(padded, filter_taps, half_width):
    detectors = padded.shape[0]
    blocks = (padded.shape[1] - 2 * half_width) // (2 * half_width)
    pieces = padded.reshape(detectors, blocks + 1, 2 * half_width)
    windows = jnp.concatenate([pieces[:, :-1], pieces[:, 1:]], axis=2)
    matrix = toeplitz_block(filter_taps, half_width)
    result = jnp.einsum("dbj,dji->dbi", windows.astype(jnp.float32), matrix.astype(jnp.float32))
    return result.reshape(detectors, blocks * 2 * half_width)


def frame_rows(whitened):
    groups = whitened.shape[0] // FD
    columns = whitened.shape[1] // FT
    frame_cube = whitened.reshape(groups, FD, columns, FT).transpose(0, 2, 1, 3)
    return frame_cube.reshape(groups * columns, FD * FT)


def owner_rows(tile_owner):
    total_tiles = tile_owner.shape[0]
    same_owner = tile_owner[:, None] == tile_owner[None, :]
    earlier = jnp.arange(total_tiles)[None, :] < jnp.arange(total_tiles)[:, None]
    slot_rank = jnp.sum((same_owner & earlier).astype(jnp.int32), axis=1)
    return (tile_owner * TILE_DEV + slot_rank).astype(jnp.int32)


def project(summed, left_weight, right_weight):
    tiles_here = summed.shape[0]
    frame_cube = summed.reshape(tiles_here, FD, FT)
    partial_value = jnp.einsum("naf,jf->naj", frame_cube, right_weight, precision=lax.Precision.HIGHEST)
    result = jnp.einsum("ia,naj->nij", left_weight, partial_value, precision=lax.Precision.HIGHEST)
    return result.reshape(tiles_here, TL * TL)


def reference(time_stream, filter_taps, det_precision, left_weight, right_weight, frame_tile, tile_owner, frame_count):
    padded = jnp.pad(time_stream, ((0, 0), (HW, HW)))
    tile_index = jnp.arange(NTILES, dtype=jnp.int32)
    frame_index = jnp.arange(F_DEV, dtype=jnp.int32)
    tile_column = frame_tile[:, 0]

    def segment(totals, segment_id):
        offset = (segment_id * SPAN).astype(jnp.int32)
        window = lax.dynamic_slice(padded, (jnp.int32(0), offset), (NDET, SPAN + 2 * HW))
        filtered = apply_filter(window, filter_taps, HW).astype(jnp.bfloat16)
        whitened = jnp.dot(det_precision, filtered, preferred_element_type=jnp.float32).astype(jnp.bfloat16)
        frames = frame_rows(whitened)
        tile_ids = lax.dynamic_slice_in_dim(tile_column, (segment_id * F_DEV).astype(jnp.int32), F_DEV)
        alive_mask = frame_index < frame_count[segment_id]
        onehot = ((tile_ids[:, None] == tile_index[None, :]) & alive_mask[:, None]).astype(jnp.bfloat16)
        added = jnp.einsum("ft,fc->tc", onehot, frames, preferred_element_type=jnp.float32)
        return totals + added, None

    totals, unused = lax.scan(segment, jnp.zeros((NTILES, FD * FT), jnp.float32), jnp.arange(N_TM * N_DET, dtype=jnp.int32))
    ordered = jnp.zeros_like(totals).at[owner_rows(tile_owner)].set(totals)
    return project(ordered, left_weight, right_weight)
```

```python
import functools

import jax
import jax.numpy as jnp
from jax import lax
from jax.experimental import pallas as pl
from jax.experimental.pallas import tpu as pltpu
from jax.sharding import PartitionSpec as P

F32 = jnp.float32
BF16 = jnp.bfloat16
ANY_NT = (((1,), (1,)), ((), ()))
TN = (((0,), (0,)), ((), ()))


def iota(shape, dim):
    return lax.broadcasted_iota(jnp.int32, shape, dim)


def params(mib):
    return pltpu.CompilerParams(vmem_limit_bytes=mib << 20)


def list_kernel(count_ref, tile_ref, owner_ref, out_ref):
    owner = owner_ref[...]
    row, col = iota((256, 256), 0), iota((256, 256), 1)
    owner_col = jnp.sum(jnp.where(row == col, owner, 0), axis=1, keepdims=True)
    rank = jnp.sum(jnp.where((owner_col == owner) & (col < row), 1, 0), axis=1, keepdims=True)
    dest_col = owner_col * 2 + rank
    number = iota((256, 128), 0)
    count = count_ref[0]
    rows = []
    for r in range(8):
        tile = tile_ref[r : r + 1, :]
        dest = jnp.sum(jnp.where(number == tile, dest_col, 0), axis=0, keepdims=True)
        rows.append(jnp.where(iota((1, 128), 1) + r * 128 < count, dest, 256))
    natural = jnp.concatenate(rows, axis=0).astype(F32).astype(BF16)
    lane, place = iota((128, 1024), 0), iota((128, 1024), 1)
    wanted = ((place % 16) // 4) * 32 + (place // 128) * 4 + place % 4
    spread = jnp.dot(natural, jnp.where(lane == wanted, 1.0, 0.0).astype(BF16), preferred_element_type=F32)
    mine = iota((8, 128), 0) == iota((8, 128), 1) // 16
    picked = [
        jnp.sum(jnp.where(mine, spread[:, c * 128 : (c + 1) * 128], 0.0), axis=0, keepdims=True)
        for c in range(8)
    ]
    out_ref[...] = jnp.broadcast_to(jnp.concatenate(picked, axis=0)[None], out_ref.shape)


def butterfly(arrays, chunk):
    lane = iota(arrays[0].shape, 1)
    for bit in range(4):
        step = 1 << bit
        low = (lane // (chunk * step)) % 2 == 0
        for i in range(16):
            if i & step:
                continue
            a, b = arrays[i], arrays[i + step]
            arrays[i] = jnp.where(low, a, pltpu.roll(b, chunk * step, 1))
            arrays[i + step] = jnp.where(low, pltpu.roll(a, 128 - chunk * step, 1), b)
    return arrays


def filter_kernel(x_ref, low_ref, high_ref, taps_ref, precision_ref, b_ref, rep_ref, rows_ref, y_ref):
    me = lax.axis_index("det")
    chosen = jnp.where(iota((1024, 256), 0) - me * 32 == iota((1024, 256), 1) // 8, 1.0, 0.0).astype(BF16)
    rep_ref[...] = jnp.dot(precision_ref[...], chosen, preferred_element_type=F32).astype(BF16)
    first_half = iota((256, 128), 1) < 64
    for half in range(2):
        for g in range(2):
            dg = half * 2 + g
            rows_ref[0:8, :] = low_ref[dg].astype(F32)
            rows_ref[8 + 2048 : 16 + 2048, :] = high_ref[dg].astype(F32)
            rows_ref[8 : 8 + 2048, :] = x_ref[dg].astype(F32).reshape(2048, 128)
            for d in range(8):
                before = rows_ref[pl.ds(d, 256, stride=8), :]
                here = rows_ref[pl.ds(8 + d, 256, stride=8), :]
                after = rows_ref[pl.ds(16 + d, 256, stride=8), :]
                window = jnp.concatenate([here, jnp.where(first_half, after, before)], axis=1).astype(BF16)
                taps = jnp.broadcast_to(taps_ref[dg * 8 + d : dg * 8 + d + 1, :], (128, 256))
                matrix = pltpu.roll(taps, 192, 1, stride=1, stride_axis=0).astype(BF16)
                y_ref[g * 8 + d] = lax.dot_general(window, matrix, ANY_NT, preferred_element_type=F32)

        def chunk(i, carry):
            at = pl.multiple_of(i * 16, 16)
            out = butterfly([y_ref[e, pl.ds(at, 16), :] for e in range(16)], 8)
            for q in range(16):
                lanes = (q % 4) * 256 + half * 128
                b_ref[pl.ds(pl.multiple_of((q // 4) * 256 + at, 16), 16), lanes : lanes + 128] = out[q].astype(BF16)
            return carry

        lax.fori_loop(0, 16, chunk, 0)


def sum_kernel(list_ref, b_ref, rep_ref, out_ref, lists_ref, hot_ref, w_ref, acc_ref, rows_ref):
    lists_ref[...] = list_ref[...].T
    number = iota((256, 256), 0).astype(F32)
    acc_ref[...] = jnp.zeros_like(acc_ref)

    def group(i, carry):
        for g in range(4):
            for c in range(4):
                names = lists_ref[pl.ds(i * 16 + g * 4 + c, 1), :]
                hot_ref[g * 256 : (g + 1) * 256, c * 256 : (c + 1) * 256] = jnp.where(number == names, 1.0, 0.0).astype(BF16)
            rep = rep_ref[pl.ds(pl.multiple_of(i * 128 + g * 32, 32), 32), :]
            for f in range(8):
                w_ref[f * 32 : (f + 1) * 32, g * 256 : (g + 1) * 256] = jnp.where(
                    iota((32, 256), 1) % 8 == f, rep.astype(F32), 0.0
                ).astype(BF16)
        for n in range(4):
            cols = slice(n * 256, (n + 1) * 256)
            s = jnp.dot(hot_ref[...], b_ref[:, cols], preferred_element_type=F32).astype(BF16)
            wide = jnp.concatenate([s[g * 256 : (g + 1) * 256] for g in range(4)], axis=1)
            acc_ref[:, cols] += lax.dot_general(wide, w_ref[...], ANY_NT, preferred_element_type=F32)
        return carry

    lax.fori_loop(0, 8, group, 0)
    for t in range(8):
        rows_ref[pl.ds(t, 256, stride=8), :] = acc_ref[:, t * 128 : (t + 1) * 128]
    out_ref[...] = rows_ref[...].astype(BF16).reshape(out_ref.shape)


def tile_kernel(in_ref, left_ref, right_ref, out_ref):
    total = jnp.sum(in_ref[...].astype(F32), axis=0)
    left = left_ref[...]
    wide = jnp.concatenate([left] * 4, axis=0)
    lane_group = iota((128, 128), 0) // 32
    for t in range(2):
        frame = total[t * 8 : (t + 1) * 8]
        parts = [
            jnp.dot(
                frame,
                jnp.where(lane_group == q, wide, 0.0),
                precision=lax.Precision.HIGHEST,
                preferred_element_type=F32,
            )
            for q in range(4)
        ]
        mixed = jnp.concatenate(parts, axis=0)
        tile = lax.dot_general(
            mixed, right_ref[...], TN, precision=lax.Precision.HIGHEST, preferred_element_type=F32
        )
        out_ref[pl.ds(t, 128, stride=2), :] = tile


def vmem(n):
    return [pl.BlockSpec(memory_space=pltpu.VMEM)] * n


def make_list(frame_count, tiles, owner):
    return pl.pallas_call(
        list_kernel,
        out_shape=jax.ShapeDtypeStruct((32, 8, 128), F32),
        in_specs=[pl.BlockSpec(memory_space=pltpu.SMEM)] + vmem(2),
        out_specs=vmem(1)[0],
        compiler_params=params(16),
        cost_estimate=pl.CostEstimate(flops=4_000_000, bytes_accessed=200_000, transcendentals=0),
        name="make_list",
    )(frame_count, tiles, owner)


def make_filtered(x, low, high, taps, precision):
    return pl.pallas_call(
        filter_kernel,
        out_shape=(jax.ShapeDtypeStruct((1024, 1024), BF16), jax.ShapeDtypeStruct((1024, 256), BF16)),
        in_specs=vmem(5),
        out_specs=tuple(vmem(2)),
        scratch_shapes=[pltpu.VMEM((2064, 128), F32), pltpu.VMEM((16, 256, 128), F32)],
        compiler_params=params(40),
        cost_estimate=pl.CostEstimate(flops=5_000_000_000, bytes_accessed=7_000_000, transcendentals=0),
        name="make_filtered",
    )(x, low, high, taps, precision)


def make_sums(lists, filtered, rep):
    return pl.pallas_call(
        sum_kernel,
        out_shape=jax.ShapeDtypeStruct((128, 16, 128), BF16),
        in_specs=vmem(3),
        out_specs=vmem(1)[0],
        scratch_shapes=[
            pltpu.VMEM((128, 256), F32),
            pltpu.VMEM((1024, 1024), BF16),
            pltpu.VMEM((256, 1024), BF16),
            pltpu.VMEM((256, 1024), F32),
            pltpu.VMEM((2048, 128), F32),
        ],
        compiler_params=params(40),
        cost_estimate=pl.CostEstimate(flops=22_000_000_000, bytes_accessed=3_000_000, transcendentals=0),
        name="make_sums",
    )(lists, filtered, rep)


def make_tiles(received, left, right):
    return pl.pallas_call(
        tile_kernel,
        out_shape=jax.ShapeDtypeStruct((256, 128), F32),
        in_specs=vmem(3),
        out_specs=vmem(1)[0],
        compiler_params=params(16),
        cost_estimate=pl.CostEstimate(flops=40_000_000, bytes_accessed=700_000, transcendentals=0),
        name="make_tiles",
    )(received, left, right)


def split_rows(a):
    return a.reshape(4, 8, -1, 128).transpose(0, 2, 1, 3)


def local(time_stream, filter_taps, det_precision, left_weight, right_weight, frame_tile, tile_owner, frame_count):
    count = lax.axis_size("tm")
    forward = [(i, i + 1) for i in range(count - 1)]
    backward = [(j, i) for i, j in forward]
    low = lax.ppermute(time_stream[:, -128:], "tm", forward)
    high = lax.ppermute(time_stream[:, :128], "tm", backward)
    own = make_list(frame_count, frame_tile.reshape(8, 128), tile_owner.reshape(1, 256))
    lists = lax.all_to_all(own, "det", split_axis=0, concat_axis=0, tiled=True)
    taps = jnp.pad(filter_taps.astype(F32), ((0, 0), (0, 256 - filter_taps.shape[1])))
    filtered, rep = make_filtered(
        split_rows(time_stream), low.reshape(4, 8, 128), high.reshape(4, 8, 128), taps, det_precision
    )
    sums = make_sums(lists.reshape(256, 128), filtered, rep)
    received = lax.all_to_all(sums, ("tm", "det"), split_axis=0, concat_axis=0, tiled=True)
    right = right_weight.reshape(128, 8, 4).transpose(2, 1, 0).reshape(32, 128)
    tiles = make_tiles(received, left_weight.T, right)
    return tiles.reshape(128, 2, 128).transpose(1, 0, 2).reshape(2, 16384)


def solution(mesh):
    return jax.shard_map(
        local,
        mesh=mesh,
        in_specs=(
            P("det", "tm"),
            P("det", None),
            P(),
            P(),
            P(),
            P(("tm", "det"), None),
            P(),
            P(("tm", "det")),
        ),
        out_specs=P(("tm", "det"), None),
        check_vma=False,
    )
```

```python
import functools

import jax
import jax.numpy as jnp
from jax import lax
from jax.experimental import pallas as pl
from jax.experimental.pallas import tpu as pltpu
from jax.sharding import PartitionSpec as P

F32 = jnp.float32
BF16 = jnp.bfloat16
ANY_NT = (((1,), (1,)), ((), ()))
GROUPS = 8
TN = (((0,), (0,)), ((), ()))


def iota(shape, dim):
    return lax.broadcasted_iota(jnp.int32, shape, dim)


def params(mib):
    return pltpu.CompilerParams(vmem_limit_bytes=mib << 20)


def prepare_kernel(count_hbm, tile_hbm, owner_hbm, x_hbm, out_ref, first_ref, last_ref, count_ref, tile_ref, owner_ref, sems):
    copies = [
        pltpu.make_async_copy(count_hbm, count_ref, sems.at[0]),
        pltpu.make_async_copy(tile_hbm, tile_ref, sems.at[1]),
        pltpu.make_async_copy(owner_hbm, owner_ref, sems.at[2]),
        pltpu.make_async_copy(x_hbm.at[:, 0], first_ref, sems.at[3]),
        pltpu.make_async_copy(x_hbm.at[:, 255], last_ref, sems.at[4]),
    ]
    for copy in copies:
        copy.start()
    for copy in copies:
        copy.wait()
    owner = owner_ref[...]
    row, col = iota((256, 256), 0), iota((256, 256), 1)
    owner_col = jnp.sum(jnp.where(row == col, owner, 0), axis=1, keepdims=True)
    rank = jnp.sum(jnp.where((owner_col == owner) & (col < row), 1, 0), axis=1, keepdims=True)
    dest_col = owner_col * 2 + rank
    number = iota((256, 128), 0)
    count = count_ref[0]
    rows = []
    for r in range(8):
        tile = tile_ref[r : r + 1, :]
        dest = jnp.sum(jnp.where(number == tile, dest_col, 0), axis=0, keepdims=True)
        rows.append(jnp.where(iota((1, 128), 1) + r * 128 < count, dest, 256))
    natural = jnp.concatenate(rows, axis=0).astype(F32).astype(BF16)
    lane, place = iota((128, 1024), 0), iota((128, 1024), 1)
    wanted = ((place % 16) // 4) * 32 + (place // 128) * 4 + place % 4
    spread = jnp.dot(natural, jnp.where(lane == wanted, 1.0, 0.0).astype(BF16), preferred_element_type=F32)
    mine = iota((8, 128), 0) == iota((8, 128), 1) // 16
    picked = [
        jnp.sum(jnp.where(mine, spread[:, c * 128 : (c + 1) * 128], 0.0), axis=0, keepdims=True)
        for c in range(8)
    ]
    out_ref[...] = jnp.broadcast_to(jnp.concatenate(picked, axis=0)[None], out_ref.shape)


def butterfly(arrays, chunk):
    lane = iota(arrays[0].shape, 1)
    for bit in range(4):
        step = 1 << bit
        low = (lane // (chunk * step)) % 2 == 0
        for i in range(16):
            if i & step:
                continue
            a, b = arrays[i], arrays[i + step]
            arrays[i] = jnp.where(low, a, pltpu.roll(b, chunk * step, 1))
            arrays[i + step] = jnp.where(low, pltpu.roll(a, 128 - chunk * step, 1), b)
    return arrays


def filter_kernel(
    x_hbm, low_ref, high_ref, taps_hbm, precision_hbm, b_ref, rep_ref,
    x_ref, narrow_ref, taps_ref, precision_ref, rows_ref, y_ref, sems,
):
    taps_copy = pltpu.make_async_copy(taps_hbm, narrow_ref, sems.at[0])
    taps_copy.start()
    x_copies = [pltpu.make_async_copy(x_hbm.at[i], x_ref.at[i], sems.at[2 + i]) for i in range(4)]
    for copy in x_copies:
        copy.start()
    precision_copy = pltpu.make_async_copy(precision_hbm, precision_ref, sems.at[1])
    precision_copy.start()
    taps_copy.wait()
    taps_ref[:, :128] = narrow_ref[:, :128].astype(F32)
    last = jnp.broadcast_to(narrow_ref[:, 128:129].astype(F32), (32, 128))
    taps_ref[:, 128:] = jnp.where(iota((32, 128), 1) == 0, last, 0.0)
    first_half = iota((256, 128), 1) < 64
    for half in range(2):
        for g in range(2):
            dg = half * 2 + g
            x_copies[dg].wait()
            rows_ref[0:8, :] = low_ref[dg].astype(F32)
            rows_ref[8 + 2048 : 16 + 2048, :] = high_ref[dg].astype(F32)
            rows_ref[8 : 8 + 2048, :] = x_ref[dg].astype(F32).reshape(2048, 128)
            for d in range(8):
                before = rows_ref[pl.ds(d, 256, stride=8), :]
                here = rows_ref[pl.ds(8 + d, 256, stride=8), :]
                after = rows_ref[pl.ds(16 + d, 256, stride=8), :]
                window = jnp.concatenate([here, jnp.where(first_half, after, before)], axis=1).astype(BF16)
                taps = jnp.broadcast_to(taps_ref[dg * 8 + d : dg * 8 + d + 1, :], (128, 256))
                matrix = pltpu.roll(taps, 192, 1, stride=1, stride_axis=0).astype(BF16)
                y_ref[g * 8 + d] = lax.dot_general(window, matrix, ANY_NT, preferred_element_type=F32)

        def chunk(i, carry):
            at = pl.multiple_of(i * 128, 128)
            out = butterfly([y_ref[e, pl.ds(at, 128), :] for e in range(16)], 8)
            for q in range(16):
                lanes = (q % 4) * 256 + half * 128
                b_ref[pl.ds(pl.multiple_of((q // 4) * 256 + at, 128), 128), lanes : lanes + 128] = out[q].astype(BF16)
            return carry

        lax.fori_loop(0, 2, chunk, 0)
    me = lax.axis_index("det")
    chosen = jnp.where(iota((1024, 256), 0) - me * 32 == iota((1024, 256), 1) // 8, 1.0, 0.0).astype(BF16)
    precision_copy.wait()
    rep_ref[...] = jnp.dot(precision_ref[...], chosen, preferred_element_type=F32).astype(BF16)


def sum_kernel(list_ref, b_ref, rep_ref, out_ref, lists_ref, hot_ref, w_ref, acc_ref, rows_ref):
    lists_ref[...] = list_ref[...].T
    number = iota((256, 256), 0).astype(F32).astype(BF16)
    one, zero = jnp.ones((), BF16), jnp.zeros((), BF16)
    acc_ref[...] = jnp.zeros_like(acc_ref)

    def group(i, carry):
        for g in range(GROUPS):
            for c in range(4):
                names = lists_ref[pl.ds(i * (4 * GROUPS) + g * 4 + c, 1), :].astype(BF16)
                hot = jnp.where(number == jnp.broadcast_to(names, (256, 256)), one, zero)
                hot_ref[g * 256 : (g + 1) * 256, c * 256 : (c + 1) * 256] = hot
            rep = rep_ref[pl.ds(pl.multiple_of(i * (32 * GROUPS) + g * 32, 32), 32), :]
            for f in range(8):
                w_ref[f * 32 : (f + 1) * 32, g * 256 : (g + 1) * 256] = jnp.where(
                    iota((32, 256), 1) % 8 == f, rep.astype(F32), 0.0
                ).astype(BF16)
        for n in range(2):
            s = jnp.dot(hot_ref[...], b_ref[:, n * 512 : (n + 1) * 512], preferred_element_type=F32).astype(BF16)
            for m in range(2):
                wide = jnp.concatenate(
                    [s[g * 256 : (g + 1) * 256, m * 256 : (m + 1) * 256] for g in range(GROUPS)], axis=1
                )
                cols = slice(n * 512 + m * 256, n * 512 + m * 256 + 256)
                acc_ref[:, cols] += lax.dot_general(wide, w_ref[...], ANY_NT, preferred_element_type=F32)
        return carry

    lax.fori_loop(0, 32 // GROUPS, group, 0)
    for t in range(8):
        rows_ref[pl.ds(t, 256, stride=8), :] = acc_ref[:, t * 128 : (t + 1) * 128]
    out_ref[...] = rows_ref[...].astype(BF16).reshape(out_ref.shape)


def tile_kernel(in_ref, left_ref, right_ref, out_ref):
    total = jnp.sum(in_ref[...].astype(F32), axis=0)
    left = left_ref[...]
    wide = jnp.concatenate([left] * 4, axis=0)
    lane_group = iota((128, 128), 0) // 32
    for t in range(2):
        frame = total[t * 8 : (t + 1) * 8]
        parts = [
            jnp.dot(
                frame,
                jnp.where(lane_group == q, wide, 0.0),
                precision=lax.Precision.HIGHEST,
                preferred_element_type=F32,
            )
            for q in range(4)
        ]
        mixed = jnp.concatenate(parts, axis=0)
        tile = lax.dot_general(
            mixed, right_ref[...], TN, precision=lax.Precision.HIGHEST, preferred_element_type=F32
        )
        out_ref[pl.ds(t, 128, stride=2), :] = tile


def vmem(n):
    return [pl.BlockSpec(memory_space=pltpu.VMEM)] * n


def anywhere(n):
    return [pl.BlockSpec(memory_space=pl.ANY)] * n


def prepare(frame_count, tiles, owner, x):
    block = jax.ShapeDtypeStruct((4, 8, 128), BF16)
    return pl.pallas_call(
        prepare_kernel,
        out_shape=(jax.ShapeDtypeStruct((32, 8, 128), F32), block, block),
        in_specs=anywhere(4),
        out_specs=tuple(vmem(3)),
        scratch_shapes=[
            pltpu.SMEM((1,), jnp.int32),
            pltpu.VMEM((8, 128), jnp.int32),
            pltpu.VMEM((1, 256), jnp.int32),
            pltpu.SemaphoreType.DMA((5,)),
        ],
        compiler_params=params(60),
        cost_estimate=pl.CostEstimate(flops=4_000_000, bytes_accessed=200_000, transcendentals=0),
        name="prepare",
    )(frame_count, tiles, owner, x)


def make_filtered(x, low, high, taps, precision):
    return pl.pallas_call(
        filter_kernel,
        out_shape=(jax.ShapeDtypeStruct((1024, 1024), BF16), jax.ShapeDtypeStruct((1024, 256), BF16)),
        in_specs=anywhere(1) + vmem(2) + anywhere(2),
        out_specs=tuple(vmem(2)),
        scratch_shapes=[
            pltpu.VMEM((4, 256, 8, 128), BF16),
            pltpu.VMEM((32, 129), BF16),
            pltpu.VMEM((32, 256), F32),
            pltpu.VMEM((1024, 1024), BF16),
            pltpu.VMEM((2064, 128), F32),
            pltpu.VMEM((16, 256, 128), F32),
            pltpu.SemaphoreType.DMA((6,)),
        ],
        compiler_params=params(51),
        cost_estimate=pl.CostEstimate(flops=5_000_000_000, bytes_accessed=7_000_000, transcendentals=0),
        name="make_filtered",
    )(x, low, high, taps, precision)


def make_sums(lists, filtered, rep):
    return pl.pallas_call(
        sum_kernel,
        out_shape=jax.ShapeDtypeStruct((128, 16, 128), BF16),
        in_specs=vmem(3),
        out_specs=vmem(1)[0],
        scratch_shapes=[
            pltpu.VMEM((128, 256), F32),
            pltpu.VMEM((GROUPS * 256, 1024), BF16),
            pltpu.VMEM((256, GROUPS * 256), BF16),
            pltpu.VMEM((256, 1024), F32),
            pltpu.VMEM((2048, 128), F32),
        ],
        compiler_params=params(44),
        cost_estimate=pl.CostEstimate(flops=22_000_000_000, bytes_accessed=3_000_000, transcendentals=0),
        name="make_sums",
    )(lists, filtered, rep)


def make_tiles(received, left, right):
    return pl.pallas_call(
        tile_kernel,
        out_shape=jax.ShapeDtypeStruct((256, 128), F32),
        in_specs=vmem(3),
        out_specs=vmem(1)[0],
        compiler_params=params(16),
        cost_estimate=pl.CostEstimate(flops=40_000_000, bytes_accessed=700_000, transcendentals=0),
        name="make_tiles",
    )(received, left, right)


def split_rows(a):
    return a.reshape(4, 8, -1, 128).transpose(0, 2, 1, 3)


def local(time_stream, filter_taps, det_precision, left_weight, right_weight, frame_tile, tile_owner, frame_count):
    count = lax.axis_size("tm")
    forward = [(i, i + 1) for i in range(count - 1)]
    backward = [(j, i) for i, j in forward]
    x = split_rows(time_stream)
    own, first, last = prepare(frame_count, frame_tile.reshape(8, 128), tile_owner.reshape(1, 256), x)
    low = lax.ppermute(last, "tm", forward)
    high = lax.ppermute(first, "tm", backward)
    lists = lax.all_to_all(own, "det", split_axis=0, concat_axis=0, tiled=True)
    filtered, rep = make_filtered(x, low, high, filter_taps, det_precision)
    sums = make_sums(lists.reshape(256, 128), filtered, rep)
    received = lax.all_to_all(sums, ("tm", "det"), split_axis=0, concat_axis=0, tiled=True)
    right = right_weight.reshape(128, 8, 4).transpose(2, 1, 0).reshape(32, 128)
    tiles = make_tiles(received, left_weight.T, right)
    return tiles.reshape(128, 2, 128).transpose(1, 0, 2).reshape(2, 16384)


def solution(mesh):
    return jax.shard_map(
        local,
        mesh=mesh,
        in_specs=(
            P("det", "tm"),
            P("det", None),
            P(),
            P(),
            P(),
            P(("tm", "det"), None),
            P(),
            P(("tm", "det")),
        ),
        out_specs=P(("tm", "det"), None),
        check_vma=False,
    )
```

```python
import functools

import jax
import jax.numpy as jnp
from jax import lax
from jax.experimental import pallas as pl
from jax.experimental.pallas import tpu as pltpu
from jax.sharding import PartitionSpec as P

F32 = jnp.float32
BF16 = jnp.bfloat16
ANY_NT = (((1,), (1,)), ((), ()))
GROUPS = 8
TN = (((0,), (0,)), ((), ()))


def iota(shape, dim):
    return lax.broadcasted_iota(jnp.int32, shape, dim)


def params(mib):
    return pltpu.CompilerParams(vmem_limit_bytes=mib << 20)


def prepare_kernel(count_hbm, tile_hbm, owner_hbm, x_hbm, out_ref, first_ref, last_ref, count_ref, tile_ref, owner_ref, sems):
    copies = [
        pltpu.make_async_copy(count_hbm, count_ref, sems.at[0]),
        pltpu.make_async_copy(tile_hbm, tile_ref, sems.at[1]),
        pltpu.make_async_copy(owner_hbm, owner_ref, sems.at[2]),
        pltpu.make_async_copy(x_hbm.at[:, 0], first_ref, sems.at[3]),
        pltpu.make_async_copy(x_hbm.at[:, 255], last_ref, sems.at[4]),
    ]
    for copy in copies:
        copy.start()
    for copy in copies:
        copy.wait()
    owner = owner_ref[...]
    row, col = iota((256, 256), 0), iota((256, 256), 1)
    owner_col = jnp.sum(jnp.where(row == col, owner, 0), axis=1, keepdims=True)
    rank = jnp.sum(jnp.where((owner_col == owner) & (col < row), 1, 0), axis=1, keepdims=True)
    dest_col = owner_col * 2 + rank
    number = iota((256, 128), 0)
    count = count_ref[...]
    rows = []
    for r in range(8):
        tile = tile_ref[r : r + 1, :]
        dest = jnp.sum(jnp.where(number == tile, dest_col, 0), axis=0, keepdims=True)
        rows.append(jnp.where(iota((1, 128), 1) + r * 128 < count, dest, 256))
    natural = jnp.concatenate(rows, axis=0).astype(F32).astype(BF16)
    lane, place = iota((128, 1024), 0), iota((128, 1024), 1)
    wanted = ((place % 16) // 4) * 32 + (place // 128) * 4 + place % 4
    spread = jnp.dot(natural, jnp.where(lane == wanted, 1.0, 0.0).astype(BF16), preferred_element_type=F32)
    mine = iota((8, 128), 0) == iota((8, 128), 1) // 16
    picked = [
        jnp.sum(jnp.where(mine, spread[:, c * 128 : (c + 1) * 128], 0.0), axis=0, keepdims=True)
        for c in range(8)
    ]
    out_ref[...] = jnp.broadcast_to(jnp.concatenate(picked, axis=0)[None], out_ref.shape)


def butterfly(arrays, chunk):
    lane = iota(arrays[0].shape, 1)
    for bit in range(4):
        step = 1 << bit
        low = (lane // (chunk * step)) % 2 == 0
        for i in range(16):
            if i & step:
                continue
            a, b = arrays[i], arrays[i + step]
            arrays[i] = jnp.where(low, a, pltpu.roll(b, chunk * step, 1))
            arrays[i + step] = jnp.where(low, pltpu.roll(a, 128 - chunk * step, 1), b)
    return arrays


def filter_kernel(
    x_hbm, low_ref, high_ref, taps_hbm, precision_hbm, b_ref, rep_ref,
    x_ref, narrow_ref, taps_ref, precision_ref, rows_ref, y_ref, sems,
):
    taps_copy = pltpu.make_async_copy(taps_hbm, narrow_ref, sems.at[0])
    taps_copy.start()
    x_copies = [pltpu.make_async_copy(x_hbm.at[i], x_ref.at[i], sems.at[2 + i]) for i in range(4)]
    for copy in x_copies:
        copy.start()
    me = lax.axis_index("det")
    block = pl.multiple_of((me // 4) * 128, 128)
    precision_copy = pltpu.make_async_copy(precision_hbm.at[:, pl.ds(block, 128)], precision_ref, sems.at[1])
    precision_copy.start()
    taps_copy.wait()
    taps_ref[:, :128] = narrow_ref[:, :128].astype(F32)
    last = jnp.broadcast_to(narrow_ref[:, 128:129].astype(F32), (32, 128))
    taps_ref[:, 128:] = jnp.where(iota((32, 128), 1) == 0, last, 0.0)
    first_half = iota((256, 128), 1) < 64
    tm = lax.axis_index("tm")
    has_low = jnp.where(tm > 0, 1.0, 0.0)
    has_high = jnp.where(tm < lax.axis_size("tm") - 1, 1.0, 0.0)
    for half in range(2):
        for g in range(2):
            dg = half * 2 + g
            x_copies[dg].wait()
            rows_ref[0:8, :] = low_ref[dg].astype(F32) * has_low
            rows_ref[8 + 2048 : 16 + 2048, :] = high_ref[dg].astype(F32) * has_high
            rows_ref[8 : 8 + 2048, :] = x_ref[dg].astype(F32).reshape(2048, 128)
            for d in range(8):
                before = rows_ref[pl.ds(d, 256, stride=8), :]
                here = rows_ref[pl.ds(8 + d, 256, stride=8), :]
                after = rows_ref[pl.ds(16 + d, 256, stride=8), :]
                window = jnp.concatenate([here, jnp.where(first_half, after, before)], axis=1).astype(BF16)
                taps = jnp.broadcast_to(taps_ref[dg * 8 + d : dg * 8 + d + 1, :], (128, 256))
                matrix = pltpu.roll(taps, 192, 1, stride=1, stride_axis=0).astype(BF16)
                y_ref[g * 8 + d] = lax.dot_general(window, matrix, ANY_NT, preferred_element_type=F32)

        def chunk(i, carry):
            at = pl.multiple_of(i * 128, 128)
            out = butterfly([y_ref[e, pl.ds(at, 128), :] for e in range(16)], 8)
            for q in range(16):
                lanes = (q % 4) * 256 + half * 128
                b_ref[pl.ds(pl.multiple_of((q // 4) * 256 + at, 128), 128), lanes : lanes + 128] = out[q].astype(BF16)
            return carry

        lax.fori_loop(0, 2, chunk, 0)
    chosen = jnp.where(iota((128, 256), 0) - (me % 4) * 32 == iota((128, 256), 1) // 8, 1.0, 0.0).astype(BF16)
    precision_copy.wait()
    rep_ref[...] = jnp.dot(precision_ref[...], chosen, preferred_element_type=F32).astype(BF16)


def sum_kernel(list_ref, b_ref, rep_ref, out_ref, lists_ref, hot_ref, w_ref, acc_ref, rows_ref):
    lists_ref[...] = list_ref[...].T
    number = iota((256, 256), 0).astype(F32).astype(BF16)
    one, zero = jnp.ones((), BF16), jnp.zeros((), BF16)
    acc_ref[...] = jnp.zeros_like(acc_ref)

    def group(i, carry):
        for g in range(GROUPS):
            for c in range(4):
                names = lists_ref[pl.ds(i * (4 * GROUPS) + g * 4 + c, 1), :].astype(BF16)
                hot = jnp.where(number == jnp.broadcast_to(names, (256, 256)), one, zero)
                hot_ref[g * 256 : (g + 1) * 256, c * 256 : (c + 1) * 256] = hot
            rep = rep_ref[pl.ds(pl.multiple_of(i * (32 * GROUPS) + g * 32, 32), 32), :]
            for f in range(8):
                w_ref[f * 32 : (f + 1) * 32, g * 256 : (g + 1) * 256] = jnp.where(
                    iota((32, 256), 1) % 8 == f, rep.astype(F32), 0.0
                ).astype(BF16)
        for n in range(2):
            s = jnp.dot(hot_ref[...], b_ref[:, n * 512 : (n + 1) * 512], preferred_element_type=F32).astype(BF16)
            for m in range(2):
                wide = jnp.concatenate(
                    [s[g * 256 : (g + 1) * 256, m * 256 : (m + 1) * 256] for g in range(GROUPS)], axis=1
                )
                cols = slice(n * 512 + m * 256, n * 512 + m * 256 + 256)
                acc_ref[:, cols] += lax.dot_general(wide, w_ref[...], ANY_NT, preferred_element_type=F32)
        return carry

    lax.fori_loop(0, 32 // GROUPS, group, 0)
    for t in range(8):
        rows_ref[pl.ds(t, 256, stride=8), :] = acc_ref[:, t * 128 : (t + 1) * 128]
    out_ref[...] = rows_ref[...].astype(BF16).reshape(out_ref.shape)


def tile_kernel(in_ref, left_ref, right_ref, out_ref):
    total = jnp.sum(in_ref[...].astype(F32), axis=0)
    left = left_ref[...]
    wide = jnp.concatenate([left] * 4, axis=0)
    lane_group = iota((128, 128), 0) // 32
    for t in range(2):
        frame = total[t * 8 : (t + 1) * 8]
        parts = [
            jnp.dot(
                frame,
                jnp.where(lane_group == q, wide, 0.0),
                precision=lax.Precision.HIGHEST,
                preferred_element_type=F32,
            )
            for q in range(4)
        ]
        mixed = jnp.concatenate(parts, axis=0)
        tile = lax.dot_general(
            mixed, right_ref[...], TN, precision=lax.Precision.HIGHEST, preferred_element_type=F32
        )
        out_ref[pl.ds(t, 128, stride=2), :] = tile


def vmem(n):
    return [pl.BlockSpec(memory_space=pltpu.VMEM)] * n


def anywhere(n):
    return [pl.BlockSpec(memory_space=pl.ANY)] * n


def prepare(frame_count, tiles, owner, x):
    block = jax.ShapeDtypeStruct((4, 8, 128), BF16)
    return pl.pallas_call(
        prepare_kernel,
        out_shape=(jax.ShapeDtypeStruct((32, 8, 128), F32), block, block),
        in_specs=anywhere(4),
        out_specs=tuple(vmem(3)),
        scratch_shapes=[
            pltpu.VMEM((1, 1), jnp.int32),
            pltpu.VMEM((8, 128), jnp.int32),
            pltpu.VMEM((1, 256), jnp.int32),
            pltpu.SemaphoreType.DMA((5,)),
        ],
        compiler_params=params(60),
        cost_estimate=pl.CostEstimate(flops=4_000_000, bytes_accessed=200_000, transcendentals=0),
        name="prepare",
    )(frame_count, tiles, owner, x)


def make_filtered(x, low, high, taps, precision):
    return pl.pallas_call(
        filter_kernel,
        out_shape=(jax.ShapeDtypeStruct((1024, 1024), BF16), jax.ShapeDtypeStruct((1024, 256), BF16)),
        in_specs=anywhere(1) + vmem(2) + anywhere(2),
        out_specs=tuple(vmem(2)),
        scratch_shapes=[
            pltpu.VMEM((4, 256, 8, 128), BF16),
            pltpu.VMEM((32, 129), BF16),
            pltpu.VMEM((32, 256), F32),
            pltpu.VMEM((1024, 128), BF16),
            pltpu.VMEM((2064, 128), F32),
            pltpu.VMEM((16, 256, 128), F32),
            pltpu.SemaphoreType.DMA((6,)),
        ],
        compiler_params=params(51),
        cost_estimate=pl.CostEstimate(flops=5_000_000_000, bytes_accessed=7_000_000, transcendentals=0),
        name="make_filtered",
    )(x, low, high, taps, precision)


def make_sums(lists, filtered, rep):
    return pl.pallas_call(
        sum_kernel,
        out_shape=jax.ShapeDtypeStruct((128, 16, 128), BF16),
        in_specs=vmem(3),
        out_specs=vmem(1)[0],
        scratch_shapes=[
            pltpu.VMEM((128, 256), F32),
            pltpu.VMEM((GROUPS * 256, 1024), BF16),
            pltpu.VMEM((256, GROUPS * 256), BF16),
            pltpu.VMEM((256, 1024), F32),
            pltpu.VMEM((2048, 128), F32),
        ],
        compiler_params=params(44),
        cost_estimate=pl.CostEstimate(flops=22_000_000_000, bytes_accessed=3_000_000, transcendentals=0),
        name="make_sums",
    )(lists, filtered, rep)


def make_tiles(received, left, right):
    return pl.pallas_call(
        tile_kernel,
        out_shape=jax.ShapeDtypeStruct((256, 128), F32),
        in_specs=vmem(3),
        out_specs=vmem(1)[0],
        compiler_params=params(16),
        cost_estimate=pl.CostEstimate(flops=40_000_000, bytes_accessed=700_000, transcendentals=0),
        name="make_tiles",
    )(received, left, right)


def split_rows(a):
    return a.reshape(4, 8, -1, 128).transpose(0, 2, 1, 3)


def local(time_stream, filter_taps, det_precision, left_weight, right_weight, frame_tile, tile_owner, frame_count):
    count = lax.axis_size("tm")
    forward = [(i, (i + 1) % count) for i in range(count)]
    backward = [(j, i) for i, j in forward]
    x = split_rows(time_stream)
    own, first, last = prepare(frame_count.reshape(1, 1), frame_tile.reshape(8, 128), tile_owner.reshape(1, 256), x)
    low = lax.ppermute(last, "tm", forward)
    high = lax.ppermute(first, "tm", backward)
    lists = lax.all_to_all(own, "det", split_axis=0, concat_axis=0, tiled=True)
    filtered, rep = make_filtered(x, low, high, filter_taps, det_precision)
    sums = make_sums(lists.reshape(256, 128), filtered, rep)
    received = lax.all_to_all(sums, ("tm", "det"), split_axis=0, concat_axis=0, tiled=True)
    right = right_weight.reshape(128, 8, 4).transpose(2, 1, 0).reshape(32, 128)
    tiles = make_tiles(received, left_weight.T, right)
    return tiles.reshape(128, 2, 128).transpose(1, 0, 2).reshape(2, 16384)


def solution(mesh):
    return jax.shard_map(
        local,
        mesh=mesh,
        in_specs=(
            P("det", "tm"),
            P("det", None),
            P(),
            P(),
            P(),
            P(("tm", "det"), None),
            P(),
            P(("tm", "det")),
        ),
        out_specs=P(("tm", "det"), None),
        check_vma=False,
    )
```

```python
import functools

import jax
import jax.numpy as jnp
from jax import lax
from jax.experimental import pallas as pl
from jax.experimental.pallas import tpu as pltpu
from jax.sharding import PartitionSpec as P

F32 = jnp.float32
BF16 = jnp.bfloat16
ANY_NT = (((1,), (1,)), ((), ()))
GROUPS = 4
TN = (((0,), (0,)), ((), ()))


def iota(shape, dim):
    return lax.broadcasted_iota(jnp.int32, shape, dim)


def params(mib):
    return pltpu.CompilerParams(vmem_limit_bytes=mib << 20)


def prepare_kernel(count_hbm, tile_hbm, owner_hbm, x_hbm, out_ref, first_ref, last_ref, count_ref, tile_ref, owner_ref, sems):
    copies = [
        pltpu.make_async_copy(count_hbm, count_ref, sems.at[0]),
        pltpu.make_async_copy(tile_hbm, tile_ref, sems.at[1]),
        pltpu.make_async_copy(owner_hbm, owner_ref, sems.at[2]),
        pltpu.make_async_copy(x_hbm.at[:, 0], first_ref, sems.at[3]),
        pltpu.make_async_copy(x_hbm.at[:, 255], last_ref, sems.at[4]),
    ]
    for copy in copies:
        copy.start()
    for copy in copies:
        copy.wait()
    owner = owner_ref[...]
    row, col = iota((256, 256), 0), iota((256, 256), 1)
    owner_col = jnp.sum(jnp.where(row == col, owner, 0), axis=1, keepdims=True)
    rank = jnp.sum(jnp.where((owner_col == owner) & (col < row), 1, 0), axis=1, keepdims=True)
    dest_col = owner_col * 2 + rank
    number = iota((256, 128), 0)
    count = count_ref[...]
    rows = []
    for r in range(8):
        tile = tile_ref[r : r + 1, :]
        dest = jnp.sum(jnp.where(number == tile, dest_col, 0), axis=0, keepdims=True)
        rows.append(jnp.where(iota((1, 128), 1) + r * 128 < count, dest, 256))
    natural = jnp.concatenate(rows, axis=0).astype(F32).astype(BF16)
    lane, place = iota((128, 1024), 0), iota((128, 1024), 1)
    wanted = ((place % 16) // 4) * 32 + (place // 128) * 4 + place % 4
    spread = jnp.dot(natural, jnp.where(lane == wanted, 1.0, 0.0).astype(BF16), preferred_element_type=F32)
    mine = iota((8, 128), 0) == iota((8, 128), 1) // 16
    picked = [
        jnp.sum(jnp.where(mine, spread[:, c * 128 : (c + 1) * 128], 0.0), axis=0, keepdims=True)
        for c in range(8)
    ]
    out_ref[...] = jnp.broadcast_to(jnp.concatenate(picked, axis=0)[None], out_ref.shape)


def butterfly(arrays, chunk):
    lane = iota(arrays[0].shape, 1)
    step = 1
    while step < len(arrays):
        low = (lane // (chunk * step)) % 2 == 0
        for i in range(len(arrays)):
            if i & step:
                continue
            a, b = arrays[i], arrays[i + step]
            arrays[i] = jnp.where(low, a, pltpu.roll(b, chunk * step, 1))
            arrays[i + step] = jnp.where(low, pltpu.roll(a, 128 - chunk * step, 1), b)
        step *= 2
    return arrays


def filter_kernel(
    x_hbm, low_ref, high_ref, taps_hbm, precision_hbm, own_ref, send_ref, rep_ref,
    x_ref, narrow_ref, taps_ref, precision_ref, rows_ref, y_ref, sems,
):
    taps_copy = pltpu.make_async_copy(taps_hbm, narrow_ref, sems.at[0])
    taps_copy.start()
    x_copies = [pltpu.make_async_copy(x_hbm.at[i], x_ref.at[i], sems.at[2 + i]) for i in range(4)]
    for copy in x_copies:
        copy.start()
    chip, core = lax.axis_index("chip"), lax.axis_index("core")
    block = pl.multiple_of((chip // 2) * 128, 128)
    precision_copy = pltpu.make_async_copy(precision_hbm.at[:, pl.ds(block, 128)], precision_ref, sems.at[1])
    precision_copy.start()
    taps_copy.wait()
    taps_ref[:, :128] = narrow_ref[:, :128].astype(F32)
    last = jnp.broadcast_to(narrow_ref[:, 128:129].astype(F32), (32, 128))
    taps_ref[:, 128:] = jnp.where(iota((32, 128), 1) == 0, last, 0.0)
    first_half = iota((256, 128), 1) < 64
    tm = lax.axis_index("tm")
    has_low = jnp.where(tm > 0, 1.0, 0.0)
    has_high = jnp.where(tm < lax.axis_size("tm") - 1, 1.0, 0.0)
    for dg in range(4):
        x_copies[dg].wait()
        rows_ref[0:8, :] = low_ref[dg].astype(F32) * has_low
        rows_ref[8 + 2048 : 16 + 2048, :] = high_ref[dg].astype(F32) * has_high
        rows_ref[8 : 8 + 2048, :] = x_ref[dg].astype(F32).reshape(2048, 128)
        for d in range(8):
            before = rows_ref[pl.ds(d, 256, stride=8), :]
            here = rows_ref[pl.ds(8 + d, 256, stride=8), :]
            after = rows_ref[pl.ds(16 + d, 256, stride=8), :]
            window = jnp.concatenate([here, jnp.where(first_half, after, before)], axis=1).astype(BF16)
            taps = jnp.broadcast_to(taps_ref[dg * 8 + d : dg * 8 + d + 1, :], (128, 256))
            matrix = pltpu.roll(taps, 192, 1, stride=1, stride_axis=0).astype(BF16)
            y = lax.dot_general(window, matrix, ANY_NT, preferred_element_type=F32)
            y_ref[dg * 8 + d] = y.reshape(16, 2, 8, 128)
    for parity, to_ref in ((1 - core, send_ref), (core, own_ref)):

        def chunk(i, carry, parity=parity, to_ref=to_ref):
            out = butterfly([y_ref[e, pl.ds(i * 8, 8), parity].reshape(64, 128) for e in range(32)], 4)
            for q in range(32):
                at = pl.multiple_of((q // 8) * 128 + i * 64, 64)
                to_ref[pl.ds(at, 64), (q % 8) * 128 : (q % 8 + 1) * 128] = out[q].astype(BF16)
            return carry

        lax.fori_loop(0, 2, chunk, 0)
    place = iota((128, 256), 1)
    wanted = (chip % 2) * 64 + ((core + place // 128) % 2) * 32 + (place % 128) // 4
    chosen = jnp.where(iota((128, 256), 0) == wanted, 1.0, 0.0).astype(BF16)
    precision_copy.wait()
    rep_ref[...] = jnp.dot(precision_ref[...], chosen, preferred_element_type=F32).astype(BF16)


def turn_kernel(list_ref, out_ref):
    out_ref[...] = list_ref[...].T


def sum_kernel(lists_ref, own_ref, other_ref, rep_ref, out_ref, hot_ref, w_ref, v_ref, acc_ref, rows_ref):
    number = iota((256, 128), 0).astype(F32).astype(BF16)
    one, zero = jnp.ones((), BF16), jnp.zeros((), BF16)
    acc_ref[...] = jnp.zeros_like(acc_ref)

    def group(i, carry):
        for g in range(GROUPS):
            for c in range(4):
                names = lists_ref[pl.ds(i * (4 * GROUPS) + g * 4 + c, 1), :].astype(BF16)
                hot = jnp.where(number == jnp.broadcast_to(names, (256, 128)), one, zero)
                at = g * 512 + c * 128
                hot_ref[:, at : at + 128] = hot
            rep = rep_ref[pl.ds(pl.multiple_of(i * (32 * GROUPS) + g * 32, 32), 32), :]
            for f in range(4):
                w_ref[g * 128 + f * 32 : g * 128 + (f + 1) * 32, :] = jnp.where(
                    iota((32, 256), 1) % 4 == f, rep.astype(F32), 0.0
                ).astype(BF16)
        for h in range(8):
            cols = slice(h * 128, (h + 1) * 128)
            both = jnp.concatenate([own_ref[:, cols], other_ref[:, cols]], axis=1)
            v = lax.dot_general(both, w_ref[...], ANY_NT, preferred_element_type=F32).astype(BF16)
            for g in range(GROUPS):
                v_ref[g * 512 : (g + 1) * 512, cols] = v[:, g * 128 : (g + 1) * 128]
        acc_ref[...] += jnp.dot(hot_ref[...], v_ref[...], preferred_element_type=F32)
        return carry

    lax.fori_loop(0, 32 // GROUPS, group, 0)
    for t in range(8):
        rows_ref[pl.ds(t, 256, stride=8), :] = acc_ref[:, t * 128 : (t + 1) * 128]
    out_ref[...] = rows_ref[...].astype(BF16).reshape(out_ref.shape)


def tile_kernel(in_ref, left_ref, right_ref, out_ref):
    total = jnp.sum(in_ref[...].astype(F32), axis=0)
    left = left_ref[...]
    wide = jnp.concatenate([left] * 4, axis=0)
    lane_group = iota((128, 128), 0) // 32
    for t in range(2):
        frame = total[t * 8 : (t + 1) * 8]
        parts = [
            jnp.dot(
                frame,
                jnp.where(lane_group == q, wide, 0.0),
                precision=lax.Precision.HIGHEST,
                preferred_element_type=F32,
            )
            for q in range(4)
        ]
        mixed = jnp.concatenate(parts, axis=0)
        tile = lax.dot_general(
            mixed, right_ref[...], TN, precision=lax.Precision.HIGHEST, preferred_element_type=F32
        )
        out_ref[pl.ds(t, 128, stride=2), :] = tile


def vmem(n):
    return [pl.BlockSpec(memory_space=pltpu.VMEM)] * n


def anywhere(n):
    return [pl.BlockSpec(memory_space=pl.ANY)] * n


def prepare(frame_count, tiles, owner, x):
    block = jax.ShapeDtypeStruct((4, 8, 128), BF16)
    return pl.pallas_call(
        prepare_kernel,
        out_shape=(jax.ShapeDtypeStruct((16, 8, 128), F32), block, block),
        in_specs=anywhere(4),
        out_specs=tuple(vmem(3)),
        scratch_shapes=[
            pltpu.VMEM((1, 1), jnp.int32),
            pltpu.VMEM((8, 128), jnp.int32),
            pltpu.VMEM((1, 256), jnp.int32),
            pltpu.SemaphoreType.DMA((5,)),
        ],
        compiler_params=params(60),
        cost_estimate=pl.CostEstimate(flops=4_000_000, bytes_accessed=200_000, transcendentals=0),
        name="prepare",
    )(frame_count, tiles, owner, x)


def make_filtered(x, low, high, taps, precision):
    half = jax.ShapeDtypeStruct((512, 1024), BF16)
    return pl.pallas_call(
        filter_kernel,
        out_shape=(half, half, jax.ShapeDtypeStruct((1024, 256), BF16)),
        in_specs=anywhere(1) + vmem(2) + anywhere(2),
        out_specs=tuple(vmem(3)),
        scratch_shapes=[
            pltpu.VMEM((4, 256, 8, 128), BF16),
            pltpu.VMEM((32, 129), BF16),
            pltpu.VMEM((32, 256), F32),
            pltpu.VMEM((1024, 128), BF16),
            pltpu.VMEM((2064, 128), F32),
            pltpu.VMEM((32, 16, 2, 8, 128), F32),
            pltpu.SemaphoreType.DMA((6,)),
        ],
        compiler_params=params(51),
        cost_estimate=pl.CostEstimate(flops=15_000_000_000, bytes_accessed=7_000_000, transcendentals=0),
        name="make_filtered",
    )(x, low, high, taps, precision)


def turn(lists):
    return pl.pallas_call(
        turn_kernel,
        out_shape=jax.ShapeDtypeStruct((128, 128), F32),
        in_specs=vmem(1),
        out_specs=vmem(1)[0],
        compiler_params=params(44),
        cost_estimate=pl.CostEstimate(flops=40_000_000_000, bytes_accessed=130_000, transcendentals=0),
        name="turn",
    )(lists)


def make_sums(lists, own, other, rep):
    return pl.pallas_call(
        sum_kernel,
        out_shape=jax.ShapeDtypeStruct((128, 16, 128), BF16),
        in_specs=vmem(4),
        out_specs=vmem(1)[0],
        scratch_shapes=[
            pltpu.VMEM((256, GROUPS * 512), BF16),
            pltpu.VMEM((GROUPS * 128, 256), BF16),
            pltpu.VMEM((GROUPS * 512, 1024), BF16),
            pltpu.VMEM((256, 1024), F32),
            pltpu.VMEM((2048, 128), F32),
        ],
        compiler_params=params(44),
        cost_estimate=pl.CostEstimate(flops=17_000_000_000, bytes_accessed=3_000_000, transcendentals=0),
        name="make_sums",
    )(lists, own, other, rep)


def make_tiles(received, left, right):
    return pl.pallas_call(
        tile_kernel,
        out_shape=jax.ShapeDtypeStruct((256, 128), F32),
        in_specs=vmem(3),
        out_specs=vmem(1)[0],
        compiler_params=params(16),
        cost_estimate=pl.CostEstimate(flops=40_000_000, bytes_accessed=700_000, transcendentals=0),
        name="make_tiles",
    )(received, left, right)


def split_rows(a):
    return a.reshape(4, 8, -1, 128).transpose(0, 2, 1, 3)


def local(time_stream, filter_taps, det_precision, left_weight, right_weight, frame_tile, tile_owner, frame_count):
    count = lax.axis_size("tm")
    forward = [(i, (i + 1) % count) for i in range(count)]
    backward = [(j, i) for i, j in forward]
    x = split_rows(time_stream)
    own, first, last = prepare(frame_count.reshape(1, 1), frame_tile.reshape(8, 128), tile_owner.reshape(1, 256), x)
    low = lax.ppermute(last, "tm", forward)
    high = lax.ppermute(first, "tm", backward)
    lists = lax.all_to_all(own, "chip", split_axis=0, concat_axis=0, tiled=True)
    kept, sent, rep = make_filtered(x, low, high, filter_taps, det_precision)
    other = lax.ppermute(sent, "core", [(0, 1), (1, 0)])
    sums = make_sums(turn(lists.reshape(128, 128)), kept, other, rep)
    received = lax.all_to_all(sums, ("tm", "chip", "core"), split_axis=0, concat_axis=0, tiled=True)
    right = right_weight.reshape(128, 8, 4).transpose(2, 1, 0).reshape(32, 128)
    tiles = make_tiles(received, left_weight.T, right)
    return tiles.reshape(128, 2, 128).transpose(1, 0, 2).reshape(2, 16384)


def solution(mesh):
    devices = mesh.devices
    split = jax.sharding.Mesh(devices.reshape(devices.shape[0], -1, 2), ("tm", "chip", "core"))
    det = ("chip", "core")
    every = ("tm", "chip", "core")
    return jax.shard_map(
        local,
        mesh=split,
        in_specs=(P(det, "tm"), P(det, None), P(), P(), P(), P(every, None), P(), P(every)),
        out_specs=P(every, None),
        check_vma=False,
    )
```

```python
import functools

import jax
import jax.numpy as jnp
from jax import lax
from jax.experimental import pallas as pl
from jax.experimental.pallas import tpu as pltpu
from jax.sharding import PartitionSpec as P

F32 = jnp.float32
BF16 = jnp.bfloat16
ANY_NT = (((1,), (1,)), ((), ()))
GROUPS = 8
TN = (((0,), (0,)), ((), ()))


def iota(shape, dim):
    return lax.broadcasted_iota(jnp.int32, shape, dim)


def params(mib):
    return pltpu.CompilerParams(vmem_limit_bytes=mib << 20)


def prepare_kernel(count_hbm, tile_hbm, owner_hbm, x_hbm, out_ref, first_ref, last_ref, count_ref, tile_ref, owner_ref, order_ref, sems):
    copies = [
        pltpu.make_async_copy(count_hbm, count_ref, sems.at[0]),
        pltpu.make_async_copy(tile_hbm, tile_ref, sems.at[1]),
        pltpu.make_async_copy(owner_hbm, owner_ref, sems.at[2]),
        pltpu.make_async_copy(x_hbm.at[:, 0], first_ref, sems.at[3]),
        pltpu.make_async_copy(x_hbm.at[:, 255], last_ref, sems.at[4]),
    ]
    for copy in copies:
        copy.start()
    lane, place = iota((128, 1024), 0), iota((128, 1024), 1)
    wanted = ((place % 16) // 4) * 32 + (place // 128) * 4 + place % 4
    order_ref[...] = jnp.where(lane == wanted, 1.0, 0.0).astype(BF16)
    row, col = iota((256, 256), 0), iota((256, 256), 1)
    for copy in copies[:3]:
        copy.wait()
    owner = owner_ref[...]
    owner_col = jnp.sum(jnp.where(row == col, owner, 0), axis=1, keepdims=True)
    rank = jnp.sum(jnp.where((owner_col == owner) & (col < row), 1, 0), axis=1, keepdims=True)
    dest_col = owner_col * 2 + rank
    number = iota((256, 128), 0)
    count = count_ref[...]
    rows = []
    for r in range(8):
        tile = tile_ref[r : r + 1, :]
        dest = jnp.sum(jnp.where(number == tile, dest_col, 0), axis=0, keepdims=True)
        rows.append(jnp.where(iota((1, 128), 1) + r * 128 < count, dest, 256))
    natural = jnp.concatenate(rows, axis=0).astype(F32).astype(BF16)
    spread = jnp.dot(natural, order_ref[...], preferred_element_type=F32)
    mine = iota((8, 128), 0) == iota((8, 128), 1) // 16
    picked = [
        jnp.sum(jnp.where(mine, spread[:, c * 128 : (c + 1) * 128], 0.0), axis=0, keepdims=True)
        for c in range(8)
    ]
    out_ref[...] = jnp.broadcast_to(jnp.concatenate(picked, axis=0)[None], out_ref.shape)
    for copy in copies[3:]:
        copy.wait()


def butterfly(arrays, chunk):
    lane = iota(arrays[0].shape, 1)
    for bit in range(4):
        step = 1 << bit
        low = (lane // (chunk * step)) % 2 == 0
        for i in range(16):
            if i & step:
                continue
            a, b = arrays[i], arrays[i + step]
            arrays[i] = jnp.where(low, a, pltpu.roll(b, chunk * step, 1))
            arrays[i + step] = jnp.where(low, pltpu.roll(a, 128 - chunk * step, 1), b)
    return arrays


def filter_kernel(
    x_hbm, low_ref, high_ref, taps_hbm, precision_hbm, b_ref, rep_ref,
    x_ref, narrow_ref, taps_ref, precision_ref, matrix_ref, rows_ref, y_ref, sems,
):
    taps_copy = pltpu.make_async_copy(taps_hbm, narrow_ref, sems.at[0])
    taps_copy.start()
    x_copies = [pltpu.make_async_copy(x_hbm.at[i], x_ref.at[i], sems.at[2 + i]) for i in range(4)]
    for copy in x_copies:
        copy.start()
    me = lax.axis_index("det")
    block = pl.multiple_of((me // 4) * 128, 128)
    precision_copy = pltpu.make_async_copy(precision_hbm.at[:, pl.ds(block, 128)], precision_ref, sems.at[1])
    precision_copy.start()
    taps_copy.wait()
    taps_ref[:, :128] = narrow_ref[:, :128].astype(F32)
    last = jnp.broadcast_to(narrow_ref[:, 128:129].astype(F32), (32, 128))
    taps_ref[:, 128:] = jnp.where(iota((32, 128), 1) == 0, last, 0.0)
    first_half = iota((256, 128), 1) < 64
    tm = lax.axis_index("tm")
    has_low = jnp.where(tm > 0, 1.0, 0.0)
    has_high = jnp.where(tm < lax.axis_size("tm") - 1, 1.0, 0.0)
    for d in range(32):
        taps = jnp.broadcast_to(taps_ref[d : d + 1, :], (128, 256))
        matrix_ref[d] = pltpu.roll(taps, 192, 1, stride=1, stride_axis=0).astype(BF16)
    for half in range(2):
        for g in range(2):
            dg = half * 2 + g
            x_copies[dg].wait()
            rows_ref[0:8, :] = low_ref[dg].astype(F32) * has_low
            rows_ref[8 + 2048 : 16 + 2048, :] = high_ref[dg].astype(F32) * has_high
            rows_ref[8 : 8 + 2048, :] = x_ref[dg].astype(F32).reshape(2048, 128)
            for d in range(8):
                before = rows_ref[pl.ds(d, 256, stride=8), :]
                here = rows_ref[pl.ds(8 + d, 256, stride=8), :]
                after = rows_ref[pl.ds(16 + d, 256, stride=8), :]
                window = jnp.concatenate([here, jnp.where(first_half, after, before)], axis=1).astype(BF16)
                y_ref[g * 8 + d] = lax.dot_general(
                    window, matrix_ref[dg * 8 + d], ANY_NT, preferred_element_type=F32
                )

        def chunk(i, carry):
            at = pl.multiple_of(i * 128, 128)
            out = butterfly([y_ref[e, pl.ds(at, 128), :] for e in range(16)], 8)
            for q in range(16):
                lanes = (q % 4) * 256 + half * 128
                b_ref[pl.ds(pl.multiple_of((q // 4) * 256 + at, 128), 128), lanes : lanes + 128] = out[q].astype(BF16)
            return carry

        lax.fori_loop(0, 2, chunk, 0)
    chosen = jnp.where(iota((128, 256), 0) - (me % 4) * 32 == iota((128, 256), 1) // 8, 1.0, 0.0).astype(BF16)
    precision_copy.wait()
    rep_ref[...] = jnp.dot(precision_ref[...], chosen, preferred_element_type=F32).astype(BF16)


def sum_kernel(list_ref, b_ref, rep_ref, out_ref, lists_ref, hot_ref, w_ref, acc_ref, rows_ref):
    lists_ref[...] = list_ref[...].T
    number = iota((256, 256), 0).astype(F32).astype(BF16)
    one, zero = jnp.ones((), BF16), jnp.zeros((), BF16)
    acc_ref[...] = jnp.zeros_like(acc_ref)

    def group(i, carry):
        for g in range(GROUPS):
            for c in range(4):
                names = lists_ref[pl.ds(i * (4 * GROUPS) + g * 4 + c, 1), :].astype(BF16)
                hot = jnp.where(number == jnp.broadcast_to(names, (256, 256)), one, zero)
                hot_ref[g * 256 : (g + 1) * 256, c * 256 : (c + 1) * 256] = hot
            rep = rep_ref[pl.ds(pl.multiple_of(i * (32 * GROUPS) + g * 32, 32), 32), :]
            for f in range(8):
                w_ref[f * 32 : (f + 1) * 32, g * 256 : (g + 1) * 256] = jnp.where(
                    iota((32, 256), 1) % 8 == f, rep.astype(F32), 0.0
                ).astype(BF16)
        for n in range(2):
            s = jnp.dot(hot_ref[...], b_ref[:, n * 512 : (n + 1) * 512], preferred_element_type=F32).astype(BF16)
            for m in range(2):
                wide = jnp.concatenate(
                    [s[g * 256 : (g + 1) * 256, m * 256 : (m + 1) * 256] for g in range(GROUPS)], axis=1
                )
                cols = slice(n * 512 + m * 256, n * 512 + m * 256 + 256)
                acc_ref[:, cols] += lax.dot_general(wide, w_ref[...], ANY_NT, preferred_element_type=F32)
        return carry

    lax.fori_loop(0, 32 // GROUPS, group, 0)
    for t in range(8):
        rows_ref[pl.ds(t, 256, stride=8), :] = acc_ref[:, t * 128 : (t + 1) * 128]
    out_ref[...] = rows_ref[...].astype(BF16).reshape(out_ref.shape)


def tile_kernel(in_ref, left_ref, right_ref, out_ref):
    total = jnp.sum(in_ref[...].astype(F32), axis=0)
    left = left_ref[...]
    wide = jnp.concatenate([left] * 4, axis=0)
    lane_group = iota((128, 128), 0) // 32
    spread = jnp.concatenate([jnp.where(lane_group == q, wide, 0.0) for q in range(4)], axis=1)
    parts = jnp.dot(total, spread, precision=lax.Precision.HIGHEST, preferred_element_type=F32)
    for t in range(2):
        mixed = jnp.concatenate([parts[t * 8 : (t + 1) * 8, q * 128 : (q + 1) * 128] for q in range(4)], axis=0)
        tile = lax.dot_general(
            mixed, right_ref[...], TN, precision=lax.Precision.HIGHEST, preferred_element_type=F32
        )
        out_ref[pl.ds(t, 128, stride=2), :] = tile


def vmem(n):
    return [pl.BlockSpec(memory_space=pltpu.VMEM)] * n


def anywhere(n):
    return [pl.BlockSpec(memory_space=pl.ANY)] * n


def prepare(frame_count, tiles, owner, x):
    block = jax.ShapeDtypeStruct((4, 8, 128), BF16)
    return pl.pallas_call(
        prepare_kernel,
        out_shape=(jax.ShapeDtypeStruct((32, 8, 128), F32), block, block),
        in_specs=anywhere(4),
        out_specs=tuple(vmem(3)),
        scratch_shapes=[
            pltpu.VMEM((1, 1), jnp.int32),
            pltpu.VMEM((8, 128), jnp.int32),
            pltpu.VMEM((1, 256), jnp.int32),
            pltpu.VMEM((128, 1024), BF16),
            pltpu.SemaphoreType.DMA((5,)),
        ],
        compiler_params=params(60),
        cost_estimate=pl.CostEstimate(flops=4_000_000, bytes_accessed=200_000, transcendentals=0),
        name="prepare",
    )(frame_count, tiles, owner, x)


def make_filtered(x, low, high, taps, precision):
    return pl.pallas_call(
        filter_kernel,
        out_shape=(jax.ShapeDtypeStruct((1024, 1024), BF16), jax.ShapeDtypeStruct((1024, 256), BF16)),
        in_specs=anywhere(1) + vmem(2) + anywhere(2),
        out_specs=tuple(vmem(2)),
        scratch_shapes=[
            pltpu.VMEM((4, 256, 8, 128), BF16),
            pltpu.VMEM((32, 129), BF16),
            pltpu.VMEM((32, 256), F32),
            pltpu.VMEM((1024, 128), BF16),
            pltpu.VMEM((32, 128, 256), BF16),
            pltpu.VMEM((2064, 128), F32),
            pltpu.VMEM((16, 256, 128), F32),
            pltpu.SemaphoreType.DMA((6,)),
        ],
        compiler_params=params(51),
        cost_estimate=pl.CostEstimate(flops=5_000_000_000, bytes_accessed=7_000_000, transcendentals=0),
        name="make_filtered",
    )(x, low, high, taps, precision)


def make_sums(lists, filtered, rep):
    return pl.pallas_call(
        sum_kernel,
        out_shape=jax.ShapeDtypeStruct((128, 16, 128), BF16),
        in_specs=vmem(3),
        out_specs=vmem(1)[0],
        scratch_shapes=[
            pltpu.VMEM((128, 256), F32),
            pltpu.VMEM((GROUPS * 256, 1024), BF16),
            pltpu.VMEM((256, GROUPS * 256), BF16),
            pltpu.VMEM((256, 1024), F32),
            pltpu.VMEM((2048, 128), F32),
        ],
        compiler_params=params(44),
        cost_estimate=pl.CostEstimate(flops=22_000_000_000, bytes_accessed=3_000_000, transcendentals=0),
        name="make_sums",
    )(lists, filtered, rep)


def make_tiles(received, left, right):
    return pl.pallas_call(
        tile_kernel,
        out_shape=jax.ShapeDtypeStruct((256, 128), F32),
        in_specs=vmem(3),
        out_specs=vmem(1)[0],
        compiler_params=params(16),
        cost_estimate=pl.CostEstimate(flops=40_000_000, bytes_accessed=700_000, transcendentals=0),
        name="make_tiles",
    )(received, left, right)


def split_rows(a):
    return a.reshape(4, 8, -1, 128).transpose(0, 2, 1, 3)


def local(time_stream, filter_taps, det_precision, left_weight, right_weight, frame_tile, tile_owner, frame_count):
    count = lax.axis_size("tm")
    forward = [(i, (i + 1) % count) for i in range(count)]
    backward = [(j, i) for i, j in forward]
    x = split_rows(time_stream)
    own, first, last = prepare(frame_count.reshape(1, 1), frame_tile.reshape(8, 128), tile_owner.reshape(1, 256), x)
    low = lax.ppermute(last, "tm", forward)
    high = lax.ppermute(first, "tm", backward)
    lists = lax.all_to_all(own, "det", split_axis=0, concat_axis=0, tiled=True)
    filtered, rep = make_filtered(x, low, high, filter_taps, det_precision)
    sums = make_sums(lists.reshape(256, 128), filtered, rep)
    received = lax.all_to_all(sums, ("tm", "det"), split_axis=0, concat_axis=0, tiled=True)
    right = right_weight.reshape(128, 8, 4).transpose(2, 1, 0).reshape(32, 128)
    tiles = make_tiles(received, left_weight.T, right)
    return tiles.reshape(128, 2, 128).transpose(1, 0, 2).reshape(2, 16384)


def solution(mesh):
    return jax.shard_map(
        local,
        mesh=mesh,
        in_specs=(
            P("det", "tm"),
            P("det", None),
            P(),
            P(),
            P(),
            P(("tm", "det"), None),
            P(),
            P(("tm", "det")),
        ),
        out_specs=P(("tm", "det"), None),
        check_vma=False,
    )
```

```python
import functools

import jax
import jax.numpy as jnp
from jax import lax
from jax.experimental import pallas as pl
from jax.experimental.pallas import tpu as pltpu
from jax.sharding import PartitionSpec as P

F32 = jnp.float32
BF16 = jnp.bfloat16
ANY_NT = (((1,), (1,)), ((), ()))
GROUPS = 4
TN = (((0,), (0,)), ((), ()))


def iota(shape, dim):
    return lax.broadcasted_iota(jnp.int32, shape, dim)


def params(mib):
    return pltpu.CompilerParams(vmem_limit_bytes=mib << 20)


def prepare_kernel(count_hbm, tile_hbm, owner_hbm, x_hbm, out_ref, first_ref, last_ref, count_ref, tile_ref, owner_ref, order_ref, sems):
    copies = [
        pltpu.make_async_copy(count_hbm, count_ref, sems.at[0]),
        pltpu.make_async_copy(tile_hbm, tile_ref, sems.at[1]),
        pltpu.make_async_copy(owner_hbm, owner_ref, sems.at[2]),
        pltpu.make_async_copy(x_hbm.at[:, 0], first_ref, sems.at[3]),
        pltpu.make_async_copy(x_hbm.at[:, 255], last_ref, sems.at[4]),
    ]
    for copy in copies:
        copy.start()
    lane, place = iota((128, 1024), 0), iota((128, 1024), 1)
    wanted = ((place % 16) // 4) * 32 + (place // 128) * 4 + place % 4
    order_ref[...] = jnp.where(lane == wanted, 1.0, 0.0).astype(BF16)
    row, col = iota((256, 256), 0), iota((256, 256), 1)
    for copy in copies[:3]:
        copy.wait()
    owner = owner_ref[...]
    owner_col = jnp.sum(jnp.where(row == col, owner, 0), axis=1, keepdims=True)
    rank = jnp.sum(jnp.where((owner_col == owner) & (col < row), 1, 0), axis=1, keepdims=True)
    dest_col = owner_col * 2 + rank
    number = iota((256, 128), 0)
    count = count_ref[...]
    rows = []
    for r in range(8):
        tile = tile_ref[r : r + 1, :]
        dest = jnp.sum(jnp.where(number == tile, dest_col, 0), axis=0, keepdims=True)
        rows.append(jnp.where(iota((1, 128), 1) + r * 128 < count, dest, 256))
    natural = jnp.concatenate(rows, axis=0).astype(F32).astype(BF16)
    spread = jnp.dot(natural, order_ref[...], preferred_element_type=F32)
    mine = iota((8, 128), 0) == iota((8, 128), 1) // 16
    picked = [
        jnp.sum(jnp.where(mine, spread[:, c * 128 : (c + 1) * 128], 0.0), axis=0, keepdims=True)
        for c in range(8)
    ]
    out_ref[...] = jnp.broadcast_to(jnp.concatenate(picked, axis=0)[None], out_ref.shape)
    for copy in copies[3:]:
        copy.wait()


def butterfly(arrays, chunk):
    lane = iota(arrays[0].shape, 1)
    for bit in range(4):
        step = 1 << bit
        low = (lane // (chunk * step)) % 2 == 0
        for i in range(16):
            if i & step:
                continue
            a, b = arrays[i], arrays[i + step]
            arrays[i] = jnp.where(low, a, pltpu.roll(b, chunk * step, 1))
            arrays[i + step] = jnp.where(low, pltpu.roll(a, 128 - chunk * step, 1), b)
    return arrays


def filter_kernel(
    x_hbm, low_ref, high_ref, taps_hbm, precision_hbm, b_ref, rep_ref,
    x_ref, narrow_ref, taps_ref, precision_ref, matrix_ref, rows_ref, y_ref, sems,
):
    taps_copy = pltpu.make_async_copy(taps_hbm, narrow_ref, sems.at[0])
    taps_copy.start()
    x_copies = [pltpu.make_async_copy(x_hbm.at[i], x_ref.at[i], sems.at[2 + i]) for i in range(4)]
    for copy in x_copies:
        copy.start()
    me = lax.axis_index("det")
    block = pl.multiple_of((me // 4) * 128, 128)
    precision_copy = pltpu.make_async_copy(precision_hbm.at[:, pl.ds(block, 128)], precision_ref, sems.at[1])
    precision_copy.start()
    taps_copy.wait()
    taps_ref[:, :128] = narrow_ref[:, :128].astype(F32)
    last = jnp.broadcast_to(narrow_ref[:, 128:129].astype(F32), (32, 128))
    taps_ref[:, 128:] = jnp.where(iota((32, 128), 1) == 0, last, 0.0)
    first_half = iota((256, 128), 1) < 64
    tm = lax.axis_index("tm")
    has_low = jnp.where(tm > 0, 1.0, 0.0)
    has_high = jnp.where(tm < lax.axis_size("tm") - 1, 1.0, 0.0)
    for d in range(32):
        taps = jnp.broadcast_to(taps_ref[d : d + 1, :], (128, 256))
        matrix_ref[d] = pltpu.roll(taps, 192, 1, stride=1, stride_axis=0).astype(BF16)
    for half in range(2):
        for g in range(2):
            dg = half * 2 + g
            x_copies[dg].wait()
            rows_ref[0:8, :] = low_ref[dg].astype(F32) * has_low
            rows_ref[8 + 2048 : 16 + 2048, :] = high_ref[dg].astype(F32) * has_high
            rows_ref[8 : 8 + 2048, :] = x_ref[dg].astype(F32).reshape(2048, 128)
            for d in range(8):
                before = rows_ref[pl.ds(d, 256, stride=8), :]
                here = rows_ref[pl.ds(8 + d, 256, stride=8), :]
                after = rows_ref[pl.ds(16 + d, 256, stride=8), :]
                window = jnp.concatenate([here, jnp.where(first_half, after, before)], axis=1).astype(BF16)
                y_ref[g * 8 + d] = lax.dot_general(
                    window, matrix_ref[dg * 8 + d], ANY_NT, preferred_element_type=F32
                )

        def chunk(i, carry):
            at = pl.multiple_of(i * 128, 128)
            out = butterfly([y_ref[e, pl.ds(at, 128), :] for e in range(16)], 8)
            for q in range(16):
                lanes = (q % 4) * 256 + half * 128
                b_ref[pl.ds(pl.multiple_of((q // 4) * 256 + at, 128), 128), lanes : lanes + 128] = out[q].astype(BF16)
            return carry

        lax.fori_loop(0, 2, chunk, 0)
    chosen = jnp.where(iota((128, 256), 0) - (me % 4) * 32 == iota((128, 256), 1) // 8, 1.0, 0.0).astype(BF16)
    precision_copy.wait()
    rep_ref[...] = jnp.dot(precision_ref[...], chosen, preferred_element_type=F32).astype(BF16)


def sum_kernel(list_ref, b_ref, rep_ref, out_ref, lists_ref, hot_ref, w_ref, acc_ref, rows_ref):
    lists_ref[...] = list_ref[...].T
    number = iota((256, 256), 0).astype(F32).astype(BF16)
    one, zero = jnp.ones((), BF16), jnp.zeros((), BF16)

    def group(i):
        for g in range(GROUPS):
            for c in range(4):
                names = lists_ref[pl.ds(i * (4 * GROUPS) + g * 4 + c, 1), :].astype(BF16)
                hot = jnp.where(number == jnp.broadcast_to(names, (256, 256)), one, zero)
                hot_ref[i % 2, g * 256 : (g + 1) * 256, c * 256 : (c + 1) * 256] = hot
            rep = rep_ref[pl.ds(pl.multiple_of(i * (32 * GROUPS) + g * 32, 32), 32), :]
            for f in range(8):
                w_ref[i % 2, f * 32 : (f + 1) * 32, g * 256 : (g + 1) * 256] = jnp.where(
                    iota((32, 256), 1) % 8 == f, rep.astype(F32), 0.0
                ).astype(BF16)
        for n in range(2):
            s = jnp.dot(hot_ref[i % 2], b_ref[:, n * 512 : (n + 1) * 512], preferred_element_type=F32).astype(BF16)
            for m in range(2):
                wide = jnp.concatenate(
                    [s[g * 256 : (g + 1) * 256, m * 256 : (m + 1) * 256] for g in range(GROUPS)], axis=1
                )
                cols = slice(n * 512 + m * 256, n * 512 + m * 256 + 256)
                part = lax.dot_general(wide, w_ref[i % 2], ANY_NT, preferred_element_type=F32)
                acc_ref[:, cols] = part if i == 0 else acc_ref[:, cols] + part

    for i in range(32 // GROUPS):
        group(i)
    for t in range(8):
        rows_ref[pl.ds(t, 256, stride=8), :] = acc_ref[:, t * 128 : (t + 1) * 128]
    out_ref[...] = rows_ref[...].astype(BF16).reshape(out_ref.shape)


def tile_kernel(in_ref, left_ref, right_ref, out_ref):
    total = jnp.sum(in_ref[...].astype(F32), axis=0)
    left = left_ref[...]
    wide = jnp.concatenate([left] * 4, axis=0)
    lane_group = iota((128, 128), 0) // 32
    spread = jnp.concatenate([jnp.where(lane_group == q, wide, 0.0) for q in range(4)], axis=1)
    parts = jnp.dot(total, spread, precision=lax.Precision.HIGHEST, preferred_element_type=F32)
    for t in range(2):
        mixed = jnp.concatenate([parts[t * 8 : (t + 1) * 8, q * 128 : (q + 1) * 128] for q in range(4)], axis=0)
        tile = lax.dot_general(
            mixed, right_ref[...], TN, precision=lax.Precision.HIGHEST, preferred_element_type=F32
        )
        out_ref[pl.ds(t, 128, stride=2), :] = tile


def vmem(n):
    return [pl.BlockSpec(memory_space=pltpu.VMEM)] * n


def anywhere(n):
    return [pl.BlockSpec(memory_space=pl.ANY)] * n


def prepare(frame_count, tiles, owner, x):
    block = jax.ShapeDtypeStruct((4, 8, 128), BF16)
    return pl.pallas_call(
        prepare_kernel,
        out_shape=(jax.ShapeDtypeStruct((32, 8, 128), F32), block, block),
        in_specs=anywhere(4),
        out_specs=tuple(vmem(3)),
        scratch_shapes=[
            pltpu.VMEM((1, 1), jnp.int32),
            pltpu.VMEM((8, 128), jnp.int32),
            pltpu.VMEM((1, 256), jnp.int32),
            pltpu.VMEM((128, 1024), BF16),
            pltpu.SemaphoreType.DMA((5,)),
        ],
        compiler_params=params(60),
        cost_estimate=pl.CostEstimate(flops=4_000_000, bytes_accessed=200_000, transcendentals=0),
        name="prepare",
    )(frame_count, tiles, owner, x)


def make_filtered(x, low, high, taps, precision):
    return pl.pallas_call(
        filter_kernel,
        out_shape=(jax.ShapeDtypeStruct((1024, 1024), BF16), jax.ShapeDtypeStruct((1024, 256), BF16)),
        in_specs=anywhere(1) + vmem(2) + anywhere(2),
        out_specs=tuple(vmem(2)),
        scratch_shapes=[
            pltpu.VMEM((4, 256, 8, 128), BF16),
            pltpu.VMEM((32, 129), BF16),
            pltpu.VMEM((32, 256), F32),
            pltpu.VMEM((1024, 128), BF16),
            pltpu.VMEM((32, 128, 256), BF16),
            pltpu.VMEM((2064, 128), F32),
            pltpu.VMEM((16, 256, 128), F32),
            pltpu.SemaphoreType.DMA((6,)),
        ],
        compiler_params=params(51),
        cost_estimate=pl.CostEstimate(flops=5_000_000_000, bytes_accessed=7_000_000, transcendentals=0),
        name="make_filtered",
    )(x, low, high, taps, precision)


def make_sums(lists, filtered, rep):
    return pl.pallas_call(
        sum_kernel,
        out_shape=jax.ShapeDtypeStruct((128, 16, 128), BF16),
        in_specs=vmem(3),
        out_specs=vmem(1)[0],
        scratch_shapes=[
            pltpu.VMEM((128, 256), F32),
            pltpu.VMEM((2, GROUPS * 256, 1024), BF16),
            pltpu.VMEM((2, 256, GROUPS * 256), BF16),
            pltpu.VMEM((256, 1024), F32),
            pltpu.VMEM((2048, 128), F32),
        ],
        compiler_params=params(44),
        cost_estimate=pl.CostEstimate(flops=22_000_000_000, bytes_accessed=3_000_000, transcendentals=0),
        name="make_sums",
    )(lists, filtered, rep)


def make_tiles(received, left, right):
    return pl.pallas_call(
        tile_kernel,
        out_shape=jax.ShapeDtypeStruct((256, 128), F32),
        in_specs=vmem(3),
        out_specs=vmem(1)[0],
        compiler_params=params(16),
        cost_estimate=pl.CostEstimate(flops=40_000_000, bytes_accessed=700_000, transcendentals=0),
        name="make_tiles",
    )(received, left, right)


def split_rows(a):
    return a.reshape(4, 8, -1, 128).transpose(0, 2, 1, 3)


def local(time_stream, filter_taps, det_precision, left_weight, right_weight, frame_tile, tile_owner, frame_count):
    count = lax.axis_size("tm")
    forward = [(i, (i + 1) % count) for i in range(count)]
    backward = [(j, i) for i, j in forward]
    x = split_rows(time_stream)
    own, first, last = prepare(frame_count.reshape(1, 1), frame_tile.reshape(8, 128), tile_owner.reshape(1, 256), x)
    low = lax.ppermute(last, "tm", forward)
    high = lax.ppermute(first, "tm", backward)
    lists = lax.all_to_all(own, "det", split_axis=0, concat_axis=0, tiled=True)
    filtered, rep = make_filtered(x, low, high, filter_taps, det_precision)
    sums = make_sums(lists.reshape(256, 128), filtered, rep)
    received = lax.all_to_all(sums, ("tm", "det"), split_axis=0, concat_axis=0, tiled=True)
    right = right_weight.reshape(128, 8, 4).transpose(2, 1, 0).reshape(32, 128)
    tiles = make_tiles(received, left_weight.T, right)
    return tiles.reshape(128, 2, 128).transpose(1, 0, 2).reshape(2, 16384)


def solution(mesh):
    return jax.shard_map(
        local,
        mesh=mesh,
        in_specs=(
            P("det", "tm"),
            P("det", None),
            P(),
            P(),
            P(),
            P(("tm", "det"), None),
            P(),
            P(("tm", "det")),
        ),
        out_specs=P(("tm", "det"), None),
        check_vma=False,
    )
```
